32 devices in a mesh: sample: 4 (over y, core), solver: 8 (over z, x).
Axes of the slice: x: 2, y: 2, z: 4, core: 2. Of those that a mesh axis runs over, the one named last changes fastest.
Arguments:
- other_index: int32 [11, 8192], P(None, ('sample', 'solver')), may hold values from 0 to 255
- slice_index: int32 [8192, 1], P(('sample', 'solver')), may hold values from 0 to 127; in each aligned block of 256 rows (0 to 255, 256 to 511, ...) at most 4 rows name the same one
- observed: bfloat16 [8192], P(('sample', 'solver')), may hold values from -6 to 6
- left_first: bfloat16 [256, 32], replicated, may hold values from -1 to 1
- left_cores: bfloat16 [4, 256, 32, 32], replicated, may hold values from -1 to 1
- right_cores: bfloat16 [5, 256, 32, 32], replicated, may hold values from -1 to 1
- right_last: bfloat16 [256, 32], replicated, may hold values from -1 to 1
Outputs:
- new_core: float32 [128, 1024], P(('sample', 'solver'))
- misfit: float32 [8192], P(('sample', 'solver'))
The draws below stay inside these ranges and needn't reach their ends.
Inputs may be any that keep to these rules, and one draw needn't show every extreme that they name: `slice_index`: within each device's aligned block of 256 entries no mode-6 value appears more than 4 times, and some value appears exactly 4 times.
All inputs are finite; a program needn't handle non-finite values.
Results may differ from the reference program's by a relative error of at most 0.0048.
Values may be sent and summed in bfloat16 or wider, within the bound.
A program may use at most 192 MiB of HBM per device.

```python
import math
import jax
import jax.numpy as jnp
import numpy as np
from jax import lax

RANK = 32
MODE = 256
SLICES = 128
LEFT_MID = 4
RIGHT_MID = 5
OTHER = 11
E_DEV = 256
CAP = 4
ENTRIES = 8192
N_SAMPLE = 4
N_SOLVER = 8


def with_ends(entries, key, smallest, top_value):
    spot = [jax.random.randint(jax.random.fold_in(key, axis), (), 0, length) for axis, length in enumerate(entries.shape)]
    longest = entries.shape.index(max(entries.shape))
    next_to = spot[:longest] + [(spot[longest] + 1) % entries.shape[longest]] + spot[longest + 1:]
    return entries.at[tuple(spot)].set(smallest).at[tuple(next_to)].set(top_value)


def steps_of(rng, extent, pieces, low, largest):
    level = 1.0
    for dim, shards_of in pieces:
        steps = jax.random.uniform(jax.random.fold_in(jax.random.fold_in(rng, 6), dim), (shards_of,), jnp.float32, low / len(pieces), largest / len(pieces))
        level = level * jnp.repeat(jnp.exp(steps), extent[dim] // shards_of).reshape((-1,) + (1,) * (len(extent) - 1 - dim))
    return level


def deal_out(stream_key, own, number, rows, count, top, bound, skew):
    sequence = jax.random.permutation(stream_key, count)
    crowded, usual = shares(count, rows * top, bound, skew, True), shares(count, rows * top, bound, skew, False)
    places = jnp.arange(count)

    def named(tallies, rotation):
        used = int((tallies > 0).sum())
        fixed = max(1, used // 4)
        passed = fixed + (places - fixed + rotation * (used - fixed)) % max(1, count - fixed)
        return jnp.zeros((count,), jnp.int32).at[sequence[jnp.where(places < fixed, places, passed)]].set(jnp.asarray(tallies, jnp.int32))

    tallies = jnp.where(number % 4 == 0, named(crowded, number // 4), named(usual, number - number // 4 - 1))
    mixed = jax.random.permutation(jax.random.fold_in(own, 3), count)
    giver, taker = mixed[0:count // 2 * 2:2], mixed[1:count // 2 * 2:2]
    slack = jnp.minimum(tallies[giver] - 1, bound - tallies[taker]) // 2
    slack = jnp.where((giver == sequence[0]) | (taker == sequence[0]) | (tallies[taker] == 0), 0, jnp.maximum(slack, 0))
    passed = jax.random.randint(jax.random.fold_in(own, 4), (count // 2,), 0, 1 << 20) % (slack + 1)
    tallies = tallies.at[giver].add(-passed).at[taker].add(passed)
    items = jnp.searchsorted(jnp.cumsum(tallies), jnp.arange(rows * top), side="right").astype(jnp.int32)
    table = items.reshape(top, rows).T
    table = table[jax.random.permutation(jax.random.fold_in(own, 1), rows)]
    rotation = jax.random.randint(jax.random.fold_in(own, 2), (rows, 1), 0, top)
    return jnp.take_along_axis(table, (jnp.arange(top)[None, :] + rotation) % top, axis=1)


def shares(count, total, reach, skew, full):
    weights = [(1 << 20) // math.isqrt(grade ** skew) + 1 for grade in range(1, count + 1)]
    largest = reach if full else min(reach, max(-(-total // count), total * weights[0] // sum(weights)))
    least = 1 if total - largest >= count - 1 else 0
    holding, spare = [largest] + [least] * (count - 1), total - largest - least * (count - 1)
    while spare > 0:
        movable = [i for i in range(1, count) if holding[i] < largest] or [i for i in range(1, count) if holding[i] < reach]
        mass, remaining = sum([weights[i] for i in movable]), spare
        for i in movable:
            extra = min(reach - holding[i], max(1, remaining * weights[i] // mass), spare)
            holding[i] = holding[i] + extra
            spare = spare - extra
    return np.array(holding)


def normal_values(own_key, extent, scale, bound, pieces=(), kind=jnp.bfloat16):
    entries = scale * jax.random.normal(own_key, extent, jnp.float32)
    if pieces:
        entries = entries * steps_of(own_key, extent, pieces, -0.22, 0.18)
    return jnp.clip(entries, -bound, bound).astype(kind)


def setup_inputs(seed: int = 0) -> dict:
    keys = jax.random.split(jax.random.key(seed), 8)
    other_index = with_ends(jax.random.randint(keys[0], (OTHER, ENTRIES), 0, MODE), jax.random.fold_in(keys[0], 1), 0, MODE - 1).astype(jnp.int32)
    slice_index_keys = jax.random.split(jax.random.fold_in(keys[1], 1), ENTRIES // E_DEV)
    slice_index_turns = jax.random.permutation(jax.random.fold_in(keys[1], 3), ENTRIES // E_DEV)
    slice_index = jax.vmap(lambda own, number: deal_out(jax.random.fold_in(keys[1], 2), own, number, E_DEV, SLICES, 1, CAP, 2))(slice_index_keys, slice_index_turns).reshape((ENTRIES, 1))
    observed = normal_values(keys[2], (ENTRIES,), 1.0, 6.0, ((0, 32),))
    left_first = normal_values(keys[3], (MODE, RANK), RANK ** -0.5, 1.0)
    left_cores = normal_values(keys[4], (LEFT_MID, MODE, RANK, RANK), RANK ** -0.5, 1.0)
    right_cores = normal_values(keys[5], (RIGHT_MID, MODE, RANK, RANK), RANK ** -0.5, 1.0)
    right_last = normal_values(keys[6], (MODE, RANK), RANK ** -0.5, 1.0)
    return dict(other_index=other_index, slice_index=slice_index, observed=observed, left_first=left_first, left_cores=left_cores, right_cores=right_cores, right_last=right_last)


ridge_weight = 2.0

def interfaces(index_block, left_first, left_cores, right_cores, right_last):
    left = jnp.take(left_first, index_block[0], axis=0).astype(jnp.float32)
    for level in range(left_cores.shape[0]):
        mats = jnp.take(left_cores[level], index_block[level + 1], axis=0).astype(jnp.float32)
        left = jnp.einsum('ej,ejk->ek', left, mats, precision=lax.Precision.HIGHEST)
    count_left = left_cores.shape[0]
    right = jnp.take(right_last, index_block[-1], axis=0).astype(jnp.float32)
    for level in range(right_cores.shape[0] - 1, -1, -1):
        mats = jnp.take(right_cores[level], index_block[count_left + 1 + level], axis=0).astype(jnp.float32)
        right = jnp.einsum('ejk,ek->ej', mats, right, precision=lax.Precision.HIGHEST)
    return (left.astype(jnp.bfloat16), right.astype(jnp.bfloat16))

def outer_rows(left, right):
    prod = left.astype(jnp.float32)[:, :, None] * right.astype(jnp.float32)[:, None, :]
    return prod.reshape(left.shape[0], RANK * RANK).astype(jnp.bfloat16)

def cholesky_solve(system, rhs):
    chol = jnp.linalg.cholesky(system)
    half = lax.linalg.triangular_solve(chol, rhs[..., None], left_side=True, lower=True)
    return lax.linalg.triangular_solve(chol, half, left_side=True, lower=True, transpose_a=True)[..., 0]

def reference(other_index, slice_index, observed, left_first, left_cores, right_cores, right_last):
    blocks = N_SAMPLE * N_SOLVER
    index_blocks = jnp.transpose(other_index.reshape(OTHER, blocks, E_DEV), (1, 0, 2))
    left, right = lax.map(lambda b: interfaces(b, left_first, left_cores, right_cores, right_last), index_blocks)
    left = left.reshape(ENTRIES, RANK)
    right = right.reshape(ENTRIES, RANK)
    ids = slice_index[:, 0].astype(jnp.int32)
    order = jnp.argsort(ids, stable=True)
    counts = jnp.zeros((SLICES,), jnp.int32).at[ids].add(1)
    starts = (jnp.cumsum(counts) - counts).astype(jnp.int32)
    step = 1024
    pad_left = jnp.concatenate([left[order], jnp.zeros((step, RANK), jnp.bfloat16)])
    pad_right = jnp.concatenate([right[order], jnp.zeros((step, RANK), jnp.bfloat16)])
    pad_value = jnp.concatenate([observed[order].astype(jnp.float32), jnp.zeros((step,), jnp.float32)])
    width = RANK * RANK

    def solve_one(value):
        begin = starts[value]
        total = counts[value]

        def add_block(turn, carry):
            gram, rhs = carry
            offset = (begin + turn * step).astype(jnp.int32)
            lpart = lax.dynamic_slice_in_dim(pad_left, offset, step, 0)
            rpart = lax.dynamic_slice_in_dim(pad_right, offset, step, 0)
            vpart = lax.dynamic_slice_in_dim(pad_value, offset, step, 0)
            rows = lax.optimization_barrier(outer_rows(lpart, rpart)).astype(jnp.float32)
            live = turn * step + jnp.arange(step) < total
            rows = jnp.where(live[:, None], rows, 0.0)
            vpart = jnp.where(live, vpart, 0.0)
            gram = gram + jnp.dot(rows.T, rows, precision=lax.Precision.HIGHEST)
            rhs = rhs + jnp.dot(rows.T, vpart, precision=lax.Precision.HIGHEST)
            return (gram, rhs)
        turns = (total + step - 1) // step
        gram, rhs = lax.fori_loop(0, turns, add_block, (jnp.zeros((width, width), jnp.float32), jnp.zeros((width,), jnp.float32)))
        system = gram + ridge_weight * jnp.eye(width, dtype=jnp.float32)
        return cholesky_solve(system, rhs)
    new_core = lax.map(solve_one, jnp.arange(SLICES, dtype=jnp.int32))

    def predict(block):
        lpart, rpart, idpart, vpart = block
        rows = lax.optimization_barrier(outer_rows(lpart, rpart)).astype(jnp.float32)
        picked = jnp.take(new_core, idpart, axis=0)
        return vpart.astype(jnp.float32) - jnp.sum(rows * picked, axis=1)
    misfit = lax.map(predict, (left.reshape(blocks, E_DEV, RANK), right.reshape(blocks, E_DEV, RANK), ids.reshape(blocks, E_DEV), observed.reshape(blocks, E_DEV)))
    return (new_core, misfit.reshape(ENTRIES))
```

```python
import functools

import jax
import jax.numpy as jnp
from jax import lax
from jax.experimental import pallas as pl
from jax.experimental.pallas import tpu as pltpu
from jax.sharding import PartitionSpec as P

SLICES = 128
CAP = 4
RIDGE = 2.0
LANES = 128
BLOCK = 16
MESH = pl.DeviceIdType.MESH
HIGHEST = lax.Precision.HIGHEST


def iota(shape, dim):
    return lax.broadcasted_iota(jnp.int32, shape, dim)


def one_hot(hit):
    return jnp.where(hit, 1.0, 0.0).astype(jnp.bfloat16)


def dot(a, b, dims=((1,), (0,)), precision=None):
    return lax.dot_general(
        a, b, (dims, ((), ())), precision=precision, preferred_element_type=jnp.float32
    )


def sweep(a, n):
    lane = iota((BLOCK, n), 1)
    sub = iota((BLOCK, n), 0)
    p = a[:BLOCK, :]
    for r in range(BLOCK):
        inv = 1.0 / p[r : r + 1, r : r + 1]
        col = p[:, r : r + 1]
        mod = jnp.where(lane == r, jnp.where(sub == r, 1.0, 0.0), p)
        row = mod[r : r + 1, :] * inv
        p = jnp.where(sub == r, row, mod - col * row)
    p = jnp.where(lane < BLOCK, -p, p)
    kept = jnp.where(iota(a.shape, 1) < BLOCK, 0.0, a)
    new = kept - dot(a[:, :BLOCK], p, precision=HIGHEST)
    new = jnp.concatenate([new[BLOCK:n], new[:BLOCK], new[n:]], axis=0)
    return pltpu.roll(new, n - BLOCK, 1)


def kernel(
    shape, oi, ids, obs, lf, lc, rc, rl, core_out, misfit_out,
    sbuf, rbuf, abuf, amat, send1, recv1, send2, recv2,
):
    n_solver, devices, owned, rows_per = shape
    count = oi.shape[1]
    rank = lf.shape[0]
    modes = lf.shape[1]
    n = devices * CAP
    me = lax.axis_index("sample") * n_solver + lax.axis_index("solver")

    def place(o):
        other = lax.rem(me + o, devices)
        return other, (other // n_solver, lax.rem(other, n_solver))

    barrier = pltpu.get_barrier_semaphore()

    def greet(o, c):
        pl.semaphore_signal(barrier, inc=1, device_id=place(o)[1], device_id_type=MESH)
        return c

    lax.fori_loop(1, devices, greet, 0)

    def hot(row):
        return one_hot(iota((modes, count), 0) == oi[row : row + 1, :])

    left = dot(lf[...], hot(0))
    right = dot(rl[...], hot(oi.shape[0] - 1))
    n_left, n_right = lc.shape[0], rc.shape[0]
    for level in range(max(n_left, n_right)):
        if level < n_left:
            picked = dot(lc[level], hot(level + 1)).reshape(rank, rank, count)
            left = jnp.sum(picked * left[:, None, :], axis=0)
        if level < n_right:
            at = n_right - 1 - level
            picked = dot(rc[at], hot(n_left + 1 + at)).reshape(rank, rank, count)
            right = jnp.sum(picked * right[None, :, :], axis=1)

    name = ids[...]
    same = one_hot(iota((SLICES, count), 0) == name)
    before = one_hot(iota((count, count), 0) < iota((count, count), 1))
    earlier = dot(same, before)
    slot = jnp.sum(
        jnp.where(iota((SLICES, count), 0) == name, earlier, 0.0), axis=0, keepdims=True
    ).astype(jnp.int32)
    owner = name // owned
    part = name - owner * owned
    spot = owner * rows_per + part * CAP + slot
    packed = jnp.concatenate(
        [
            left, right, jnp.broadcast_to(obs[...].astype(jnp.float32), (8, count)),
            jnp.zeros((LANES - 2 * rank - 8, count), jnp.float32),
        ],
        axis=0,
    ).astype(jnp.bfloat16)
    put = one_hot(iota((devices * rows_per, count), 0) == spot)
    sent = dot(put, packed, ((1,), (1,))).astype(jnp.bfloat16)
    sbuf[...] = sent.reshape(devices, rows_per, LANES)

    pl.semaphore_wait(barrier, devices - 1)

    def first(o):
        other, where = place(o)
        return pltpu.make_async_remote_copy(
            src_ref=sbuf.at[other], dst_ref=rbuf.at[me], send_sem=send1.at[o],
            recv_sem=recv1.at[o], device_id=where, device_id_type=MESH,
        )

    def start_first(o, c):
        first(o).start()
        return c

    def wait_first(o, c):
        first(o).wait()
        return c

    lax.fori_loop(1, devices, start_first, 0)
    rbuf[me] = sbuf[me]
    lax.fori_loop(1, devices, wait_first, 0)

    got = rbuf[...].reshape(devices * rows_per, LANES)
    spread = iota((LANES, rank * rank), 0)
    wide = iota((LANES, rank * rank), 1)
    spread_left = one_hot(spread == wide // rank)
    spread_right = one_hot(spread == rank + wide % rank)
    eye = jnp.where(iota((n, n), 0) == iota((n, n), 1), RIDGE, 0.0)
    order = iota((n, devices * rows_per), 0)
    source = iota((n, devices * rows_per), 1)
    rows = []
    for q in range(owned):
        pick = one_hot(source == (order // CAP) * rows_per + q * CAP + order % CAP)
        mine = dot(pick, got).astype(jnp.bfloat16)
        outer = (dot(mine, spread_left) * dot(mine, spread_right)).astype(jnp.bfloat16)
        rows.append(outer)
        amat[q, :n, :] = dot(outer, outer, ((1,), (1,))) + eye
        value = one_hot(iota((8, LANES), 1) == 2 * rank)
        amat[q, n:, :] = dot(value, mine, ((1,), (1,)))

    def step(t, c):
        for q in range(owned):
            amat[q] = sweep(amat[q], n)
        return c

    lax.fori_loop(0, n // BLOCK, step, 0)

    alphas = [amat[q, n : n + 1, :] for q in range(owned)]
    fill = [jnp.zeros((8 - owned, n), jnp.float32)] if owned < 8 else []
    abuf[me] = jnp.concatenate(alphas + fill, axis=0)

    def second(o):
        other, where = place(o)
        return pltpu.make_async_remote_copy(
            src_ref=abuf.at[me], dst_ref=abuf.at[me], send_sem=send2.at[o],
            recv_sem=recv2.at[o], device_id=where, device_id_type=MESH,
        )

    def start_second(o, c):
        second(o).start()
        return c

    def wait_second(o, c):
        second(o).wait()
        return c

    lax.fori_loop(1, devices, start_second, 0)
    for q in range(owned):
        alpha = jnp.broadcast_to(alphas[q], (8, n))
        core_out[q : q + 1, :] = dot(alpha, rows[q].astype(jnp.float32), precision=HIGHEST)[:1]
    lax.fori_loop(1, devices, wait_second, 0)

    table = abuf[...].reshape(devices * 8, n)
    from_row = owner * 8 + part
    pick = jnp.where(iota((devices * 8, count), 0) == from_row, 1.0, 0.0)
    lanes = dot(table, pick, ((0,), (0,)), precision=HIGHEST)
    chosen = jnp.where(iota((n, count), 0) == me * CAP + slot, lanes, 0.0)
    misfit_out[...] = RIDGE * jnp.sum(chosen, axis=0, keepdims=True)


def per_device(shape, other_index, slice_index, observed, left_first, left_cores, right_cores, right_last):
    n_solver, devices, owned, rows_per = shape
    rank = left_first.shape[1]
    modes = left_first.shape[0]
    count = observed.shape[0]
    n = devices * CAP

    def flat(cores):
        return jnp.transpose(cores, (0, 2, 3, 1)).reshape(cores.shape[0], rank * rank, modes)

    core, misfit = pl.pallas_call(
        functools.partial(kernel, shape),
        out_shape=(
            jax.ShapeDtypeStruct((owned, rank * rank), jnp.float32),
            jax.ShapeDtypeStruct((1, count), jnp.float32),
        ),
        in_specs=[pl.BlockSpec(memory_space=pltpu.VMEM)] * 7,
        out_specs=(pl.BlockSpec(memory_space=pltpu.VMEM),) * 2,
        scratch_shapes=[
            pltpu.VMEM((devices, rows_per, LANES), jnp.bfloat16),
            pltpu.VMEM((devices, rows_per, LANES), jnp.bfloat16),
            pltpu.VMEM((devices, 8, n), jnp.float32),
            pltpu.VMEM((owned, n + 8, n), jnp.float32),
            pltpu.SemaphoreType.DMA((devices,)),
            pltpu.SemaphoreType.DMA((devices,)),
            pltpu.SemaphoreType.DMA((devices,)),
            pltpu.SemaphoreType.DMA((devices,)),
        ],
        compiler_params=pltpu.CompilerParams(
            collective_id=0, has_side_effects=True, vmem_limit_bytes=48 * 1024 * 1024
        ),
    )(
        other_index, slice_index.reshape(1, count), observed.reshape(1, count), left_first.T,
        flat(left_cores), flat(right_cores), right_last.T,
    )
    return core, misfit.reshape(count)


def solution(mesh):
    n_solver = mesh.shape["solver"]
    devices = mesh.shape["sample"] * n_solver
    owned = SLICES // devices
    rows_per = -(-owned * CAP // 16) * 16
    both = ("sample", "solver")
    return jax.shard_map(
        functools.partial(per_device, (n_solver, devices, owned, rows_per)),
        mesh=mesh,
        in_specs=(P(None, both), P(both, None), P(both), P(), P(), P(), P()),
        out_specs=(P(both, None), P(both)),
        check_vma=False,
    )
```

```python
import functools

import jax
import jax.numpy as jnp
from jax import lax
from jax.experimental import pallas as pl
from jax.experimental.pallas import tpu as pltpu
from jax.sharding import PartitionSpec as P

SLICES = 128
CAP = 4
RIDGE = 2.0
LANES = 128
BLOCK = 16
MESH = pl.DeviceIdType.MESH
HIGHEST = lax.Precision.HIGHEST


def iota(shape, dim):
    return lax.broadcasted_iota(jnp.int32, shape, dim)


def one_hot(hit):
    return jnp.where(hit, 1.0, 0.0).astype(jnp.bfloat16)


def dot(a, b, dims=((1,), (0,)), precision=None):
    return lax.dot_general(
        a, b, (dims, ((), ())), precision=precision, preferred_element_type=jnp.float32
    )


def split3(x):
    first = x.astype(jnp.bfloat16)
    rest = x - first.astype(jnp.float32)
    second = rest.astype(jnp.bfloat16)
    third = (rest - second.astype(jnp.float32)).astype(jnp.bfloat16)
    return first, second, third


def update(a, p):
    a1, a2, a3 = split3(a[:, :BLOCK])
    p1, p2, p3 = split3(p)
    return dot(
        jnp.concatenate([a1, a1, a2, a2, a1, a3], axis=1),
        jnp.concatenate([p1, p2, p1, p2, p3, p1], axis=0),
    )


def sweep(a, n):
    lane = iota((BLOCK, n), 1)
    sub = iota((BLOCK, n), 0)
    p = a[:BLOCK, :]
    for r in range(0, BLOCK, 2):
        c0 = jnp.broadcast_to(p[:, r : r + 1], p.shape)
        c1 = jnp.broadcast_to(p[:, r + 1 : r + 2], p.shape)
        mod = jnp.where(lane == r, jnp.where(sub == r, 1.0, 0.0), p)
        mod = jnp.where(lane == r + 1, jnp.where(sub == r + 1, 1.0, 0.0), mod)
        inv0 = 1.0 / c0[r : r + 1, :]
        ratio = c0[r + 1 : r + 2, :] * inv0
        inv1 = 1.0 / (c1[r + 1 : r + 2, :] - ratio * c1[r : r + 1, :])
        m0, m1 = mod[r : r + 1, :], mod[r + 1 : r + 2, :]
        row1 = (m1 - ratio * m0) * inv1
        row0 = m0 * inv0 - (c1[r : r + 1, :] * inv0) * row1
        p = jnp.where(sub == r, row0, jnp.where(sub == r + 1, row1, mod - c0 * row0 - c1 * row1))
    p = jnp.where(lane < BLOCK, -p, p)
    kept = jnp.where(iota(a.shape, 1) < BLOCK, 0.0, a)
    new = kept - update(a, p)
    new = jnp.concatenate([new[BLOCK:n], new[:BLOCK], new[n:]], axis=0)
    return pltpu.roll(new, n - BLOCK, 1)


def kernel(
    shape, oi_hbm, ids_hbm, obs_hbm, lf_hbm, lc_hbm, rc_hbm, rl_hbm, core_out, misfit_out,
    oi, ids, obs, lf, lc, rc, rl, sbuf, rbuf, sbuf2, rbuf2, amat,
    load_small, load_left, load_right, send1, recv1, send2, recv2,
):
    n_solver, devices, owned, rows_per = shape
    count = oi.shape[1]
    rank = lf.shape[0]
    modes = lf.shape[1]
    n = devices * CAP
    me = lax.axis_index("sample") * n_solver + lax.axis_index("solver")

    def place(o):
        other = lax.rem(me + o, devices)
        return other, (other // n_solver, lax.rem(other, n_solver))

    barrier = pltpu.get_barrier_semaphore()

    def greet(o, c):
        pl.semaphore_signal(barrier, inc=1, device_id=place(o)[1], device_id_type=MESH)
        return c

    small = [
        pltpu.make_async_copy(a, b, load_small.at[i])
        for i, (a, b) in enumerate(
            ((oi_hbm, oi), (lf_hbm, lf), (rl_hbm, rl), (ids_hbm, ids), (obs_hbm, obs))
        )
    ]
    n_left, n_right = lc.shape[0], rc.shape[0]
    lefts = [pltpu.make_async_copy(lc_hbm.at[i], lc.at[i], load_left.at[i]) for i in range(n_left)]
    rights = [pltpu.make_async_copy(rc_hbm.at[i], rc.at[i], load_right.at[i]) for i in range(n_right)]
    for copy in small:
        copy.start()
    for level in range(max(n_left, n_right)):
        if level < n_left:
            lefts[level].start()
        if level < n_right:
            rights[n_right - 1 - level].start()
    lax.fori_loop(1, devices, greet, 0)
    for copy in small:
        copy.wait()

    def hot(row):
        return one_hot(iota((modes, count), 0) == oi[row : row + 1, :])

    left = dot(lf[...], hot(0))
    right = dot(rl[...], hot(oi.shape[0] - 1))
    for level in range(max(n_left, n_right)):
        if level < n_left:
            lefts[level].wait()
            picked = dot(lc[level], hot(level + 1)).reshape(rank, rank, count)
            left = jnp.sum(picked * left[:, None, :], axis=0)
        if level < n_right:
            at = n_right - 1 - level
            rights[at].wait()
            picked = dot(rc[at], hot(n_left + 1 + at)).reshape(rank, rank, count)
            right = jnp.sum(picked * right[None, :, :], axis=1)

    name = ids[...]
    same = one_hot(iota((SLICES, count), 0) == name)
    before = one_hot(iota((count, count), 0) < iota((count, count), 1))
    earlier = dot(same, before)
    slot = jnp.sum(
        jnp.where(iota((SLICES, count), 0) == name, earlier, 0.0), axis=0, keepdims=True
    ).astype(jnp.int32)
    owner = name // owned
    part = name - owner * owned
    spot = owner * rows_per + part * CAP + slot
    packed = jnp.concatenate(
        [
            left, right, jnp.broadcast_to(obs[...].astype(jnp.float32), (8, count)),
            jnp.zeros((LANES - 2 * rank - 8, count), jnp.float32),
        ],
        axis=0,
    ).astype(jnp.bfloat16)
    put = one_hot(iota((devices * rows_per, count), 0) == spot)
    sent = dot(put, packed, ((1,), (1,))).astype(jnp.bfloat16)
    sbuf[...] = sent.reshape(devices, rows_per, LANES)

    pl.semaphore_wait(barrier, devices - 1)

    def first(o):
        other, where = place(o)
        return pltpu.make_async_remote_copy(
            src_ref=sbuf.at[other], dst_ref=rbuf.at[me], send_sem=send1.at[o],
            recv_sem=recv1.at[o], device_id=where, device_id_type=MESH,
        )

    def start_first(o, c):
        first(o).start()
        return c

    def wait_first(o, c):
        first(o).wait()
        return c

    lax.fori_loop(1, devices, start_first, 0)
    rbuf[me] = sbuf[me]
    lax.fori_loop(1, devices, wait_first, 0)

    got = rbuf[...].reshape(devices * rows_per, LANES)
    spread = iota((LANES, rank * rank), 0)
    wide = iota((LANES, rank * rank), 1)
    spread_left = one_hot(spread == wide // rank)
    spread_right = one_hot(spread == rank + wide % rank)
    eye = jnp.where(iota((n, n), 0) == iota((n, n), 1), RIDGE, 0.0)
    order = iota((n, devices * rows_per), 0)
    source = iota((n, devices * rows_per), 1)
    rows = []
    for q in range(owned):
        pick = one_hot(source == (order // CAP) * rows_per + q * CAP + order % CAP)
        mine = dot(pick, got).astype(jnp.bfloat16)
        outer = (dot(mine, spread_left) * dot(mine, spread_right)).astype(jnp.bfloat16)
        rows.append(outer)
        amat[q, :n, :] = dot(outer, outer, ((1,), (1,))) + eye
        value = one_hot(iota((8, LANES), 1) == 2 * rank)
        amat[q, n:, :] = dot(value, mine, ((1,), (1,)))

    def step(t, c):
        for q in range(owned):
            amat[q] = sweep(amat[q], n)
        return c

    lax.fori_loop(0, n // BLOCK, step, 0)

    alphas = [amat[q, n : n + 1, :] for q in range(owned)]
    mine_of = iota((devices, n), 1) // CAP == iota((devices, n), 0)
    answers = jnp.zeros((devices, LANES), jnp.float32)
    for q in range(owned):
        to = iota((n, LANES), 1) == q * CAP + iota((n, LANES), 0) % CAP
        answers += dot(
            jnp.where(mine_of, alphas[q], 0.0), jnp.where(to, 1.0, 0.0), precision=HIGHEST
        )
    for d in range(devices):
        sbuf2[d, 0:1, :] = answers[d : d + 1, :]
    rbuf2[me] = sbuf2[me]

    def second(o):
        other, where = place(o)
        return pltpu.make_async_remote_copy(
            src_ref=sbuf2.at[other], dst_ref=rbuf2.at[me], send_sem=send2.at[o],
            recv_sem=recv2.at[o], device_id=where, device_id_type=MESH,
        )

    def start_second(o, c):
        second(o).start()
        return c

    def wait_second(o, c):
        second(o).wait()
        return c

    lax.fori_loop(1, devices, start_second, 0)
    for q in range(owned):
        alpha = jnp.broadcast_to(alphas[q], (8, n))
        core_out[q : q + 1, :] = dot(alpha, rows[q].astype(jnp.float32), precision=HIGHEST)[:1]
    lax.fori_loop(1, devices, wait_second, 0)

    table = jnp.concatenate([rbuf2[d] for d in range(devices)], axis=0)
    pick = jnp.where(iota((devices, count), 0) == owner, 1.0, 0.0)
    lanes = dot(table, pick, ((0,), (0,)), precision=HIGHEST)
    chosen = jnp.where(iota((LANES, count), 0) == part * CAP + slot, lanes, 0.0)
    misfit_out[...] = RIDGE * jnp.sum(chosen, axis=0, keepdims=True)


def per_device(shape, other_index, slice_index, observed, left_first, left_cores, right_cores, right_last):
    n_solver, devices, owned, rows_per = shape
    rank = left_first.shape[1]
    modes = left_first.shape[0]
    count = observed.shape[0]
    n = devices * CAP

    def flat(cores):
        return jnp.transpose(cores, (0, 2, 3, 1)).reshape(cores.shape[0], rank * rank, modes)

    core, misfit = pl.pallas_call(
        functools.partial(kernel, shape),
        out_shape=(
            jax.ShapeDtypeStruct((owned, rank * rank), jnp.float32),
            jax.ShapeDtypeStruct((1, count), jnp.float32),
        ),
        in_specs=[pl.BlockSpec(memory_space=pltpu.HBM)] * 7,
        out_specs=(pl.BlockSpec(memory_space=pltpu.VMEM),) * 2,
        scratch_shapes=[
            pltpu.VMEM(other_index.shape, jnp.int32),
            pltpu.VMEM((1, count), jnp.int32),
            pltpu.VMEM((1, count), jnp.bfloat16),
            pltpu.VMEM((rank, modes), jnp.bfloat16),
            pltpu.VMEM((left_cores.shape[0], rank * rank, modes), jnp.bfloat16),
            pltpu.VMEM((right_cores.shape[0], rank * rank, modes), jnp.bfloat16),
            pltpu.VMEM((rank, modes), jnp.bfloat16),
            pltpu.VMEM((devices, rows_per, LANES), jnp.bfloat16),
            pltpu.VMEM((devices, rows_per, LANES), jnp.bfloat16),
            pltpu.VMEM((devices, 1, LANES), jnp.float32),
            pltpu.VMEM((devices, 1, LANES), jnp.float32),
            pltpu.VMEM((owned, n + 8, n), jnp.float32),
            pltpu.SemaphoreType.DMA((5,)),
            pltpu.SemaphoreType.DMA((left_cores.shape[0],)),
            pltpu.SemaphoreType.DMA((right_cores.shape[0],)),
            pltpu.SemaphoreType.DMA((devices,)),
            pltpu.SemaphoreType.DMA((devices,)),
            pltpu.SemaphoreType.DMA((devices,)),
            pltpu.SemaphoreType.DMA((devices,)),
        ],
        compiler_params=pltpu.CompilerParams(
            collective_id=0, has_side_effects=True, vmem_limit_bytes=60 * 1024 * 1024
        ),
    )(
        other_index, slice_index.reshape(1, count), observed.reshape(1, count), left_first.T,
        flat(left_cores), flat(right_cores), right_last.T,
    )
    return core, misfit.reshape(count)


def solution(mesh):
    n_solver = mesh.shape["solver"]
    devices = mesh.shape["sample"] * n_solver
    owned = SLICES // devices
    rows_per = -(-owned * CAP // 16) * 16
    both = ("sample", "solver")
    return jax.shard_map(
        functools.partial(per_device, (n_solver, devices, owned, rows_per)),
        mesh=mesh,
        in_specs=(P(None, both), P(both, None), P(both), P(), P(), P(), P()),
        out_specs=(P(both, None), P(both)),
        check_vma=False,
    )
```
